32 devices in a mesh: node: 16 (over z, y, x), head: 2 (over core).
Axes of the slice: x: 2, y: 2, z: 4, core: 2. Of those that a mesh axis runs over, the one named last changes fastest.
Arguments:
- features: bfloat16 [2048, 128], P('node'), may hold values from -1201 to 1201
- proj_weight: bfloat16 [128, 1024], P(None, 'head'), may hold values from -1 to 1
- score_source: float32 [8, 128], P('head'), may hold values from -1 to 1
- score_target: float32 [8, 128], P('head'), may hold values from -1 to 1
- out_weight: bfloat16 [1024, 256], P('head'), may hold values from -0.1875 to 0.1875
- presence: int32 [16, 16], P('node'), may hold values from 0 to 1, as said below
- tile_masks: int32 [16, 4, 128, 128], P('node'), may hold values 0 or 1
Outputs:
- mixed: bfloat16 [2048, 256], P('node')
The draws below stay inside these ranges and needn't reach their ends.
Inputs may be any that keep to these rules, and one draw needn't show every extreme that they name: Each row holds exactly 4 ones; tile_masks[r, k] belongs to the k-th present tile of row r of presence, counted in ascending order of tile.
All inputs are finite; a program needn't handle non-finite values. No bound on the sum of `tile_masks` on one device may be relied on, other than what follows from the above.
Results may differ from the reference program's by a relative error of at most 0.015.
Values may be sent and summed in bfloat16 or wider, within the bound.
A program may use at most 64 MiB of HBM per device.

```python
import math
import jax
import jax.numpy as jnp
from jax import lax

D_IN = 128
HEADS = 8
HD = 128
OUT = 256
TILE = 128
NODES = 2048
TILE_COUNT = 16
TILE_SLOTS = 4


def shared_weights(key):
    weight = jax.random.truncated_normal(jax.random.fold_in(key, 31), -4.0, 4.0, (D_IN, HEADS * HD), jnp.float32) / math.sqrt(D_IN)
    source_vec = jax.random.truncated_normal(jax.random.fold_in(key, 32), -4.0, 4.0, (HEADS, HD), jnp.float32) / math.sqrt(HD)
    target_vec = jax.random.truncated_normal(jax.random.fold_in(key, 33), -4.0, 4.0, (HEADS, HD), jnp.float32) / math.sqrt(HD)
    return (weight, source_vec, target_vec)


def draw_proj_weight(key, part):
    return shared_weights(key)[0].astype(jnp.bfloat16)


def draw_score_source(key, part):
    return shared_weights(key)[1]


def draw_score_target(key, part):
    return shared_weights(key)[2]


def draw_features(key, part):
    base = jax.random.truncated_normal(jax.random.fold_in(key, 34), -6.0, 6.0, (NODES, D_IN), jnp.float32)
    return base.astype(jnp.bfloat16)


def draw_presence(key, part):
    noise_key, favour_key = jax.random.split(jax.random.fold_in(key, 21))
    noise = jax.random.randint(noise_key, (TILE_COUNT, TILE_COUNT), 0, 65536, dtype=jnp.int32)
    favour = jax.random.randint(favour_key, (1, TILE_COUNT), 1, 5, dtype=jnp.int32)
    ranking = noise * favour * TILE_COUNT + jnp.arange(TILE_COUNT, dtype=jnp.int32)[None, :]
    cutoff = lax.top_k(ranking, TILE_SLOTS)[0][:, TILE_SLOTS - 1:TILE_SLOTS]
    return (ranking >= cutoff).astype(jnp.int32)


def plant(array, stream_key, least, top_value):
    longest = array.shape.index(max(array.shape))
    spots = []
    for shift in (0, 1):
        where = [jax.random.randint(jax.random.fold_in(stream_key, axis), (), 0, length) for axis, length in enumerate(array.shape)]
        where[longest] = (where[longest] + shift) % array.shape[longest]
        spots.append(tuple(where))
    return array.at[spots[0]].set(least).at[spots[1]].set(top_value)


def block_scale(key, dims, pieces, smallest, high):
    def one(dim, blocks):
        steps = jax.random.uniform(jax.random.fold_in(jax.random.fold_in(key, 6), dim), (blocks,), jnp.float32, smallest / len(pieces), high / len(pieces))
        return jnp.repeat(jnp.exp(steps), dims[dim] // blocks).reshape((-1,) + (1,) * (len(dims) - dim - 1))

    loudness = one(*pieces[0])
    for cut in pieces[1:]:
        loudness = loudness * one(*cut)
    return loudness


def centred(stream_key, extent, deviation, most, cuts=(), kind=jnp.bfloat16):
    gain = block_scale(stream_key, extent, cuts, -0.22, 0.18) if cuts else 1.0
    values = jax.random.normal(stream_key, extent, jnp.float32) * deviation * gain
    return jnp.minimum(jnp.maximum(values, -most), most).astype(kind)


def setup_inputs(seed: int = 0) -> dict:
    arg_keys = jax.random.split(jax.random.key(seed), 8)
    return {
        "features": draw_features(jax.random.fold_in(arg_keys[7], 71), 0),
        "proj_weight": draw_proj_weight(jax.random.fold_in(arg_keys[7], 71), 0),
        "score_source": draw_score_source(jax.random.fold_in(arg_keys[7], 71), 0),
        "score_target": draw_score_target(jax.random.fold_in(arg_keys[7], 71), 0),
        "out_weight": centred(arg_keys[4], (HEADS * HD, OUT), (HEADS * HD) ** -0.5, 0.1875, ((0, 2),)),
        "presence": draw_presence(jax.random.fold_in(arg_keys[7], 71), 0),
        "tile_masks": plant((jax.random.randint(arg_keys[6], (TILE_COUNT, TILE_SLOTS, TILE, TILE), 0, 8) < 1).astype(jnp.int32), jax.random.fold_in(arg_keys[6], 1), 0, 1),
    }


def leaky_relu(values):
    return jnp.where(values > 0, values, 0.2 * values)


def reference(features, proj_weight, score_source, score_target, out_weight, presence, tile_masks):
    projected = jnp.dot(features, proj_weight, preferred_element_type=jnp.float32).astype(jnp.bfloat16)
    values = lax.optimization_barrier(projected).astype(jnp.float32).reshape(NODES, HEADS, HD)
    target_terms = jnp.sum(values * score_target[None], axis=-1)
    source_terms = jnp.sum(values * score_source[None], axis=-1)
    tile_lanes = jnp.arange(TILE, dtype=jnp.int32)

    def one_tile(row_tile):
        present_ids = jnp.nonzero(presence[row_tile], size=TILE_SLOTS)[0].astype(jnp.int32)
        source_ids = (present_ids[:, None] * TILE + tile_lanes[None, :]).reshape(TILE_SLOTS * TILE)
        target_ids = row_tile * TILE + tile_lanes
        tile_bits = jnp.transpose(tile_masks[row_tile], (1, 0, 2)).reshape(TILE, TILE_SLOTS * TILE)
        linked = (tile_bits == 1) & (source_ids[None, :] != target_ids[:, None])
        edge_scores = leaky_relu(target_terms[target_ids][:, None, :] + source_terms[source_ids][None, :, :])
        self_score = leaky_relu(target_terms[target_ids] + source_terms[target_ids])
        masked = jnp.where(linked[:, :, None], edge_scores, -jnp.inf)
        row_peak = jnp.maximum(jnp.max(masked, axis=1), self_score)
        edge_weights = jnp.where(linked[:, :, None], jnp.exp(edge_scores - row_peak[:, None, :]), 0.0)
        self_weight = jnp.exp(self_score - row_peak)
        denominator = jnp.sum(edge_weights, axis=1) + self_weight
        rounded = lax.optimization_barrier(edge_weights.astype(jnp.bfloat16)).astype(jnp.float32)
        self_rounded = lax.optimization_barrier(self_weight.astype(jnp.bfloat16)).astype(jnp.float32)
        weighted = jnp.einsum("tsh,shd->thd", rounded, values[source_ids])
        weighted = weighted + self_rounded[:, :, None] * values[target_ids]
        heads_out = jax.nn.elu(weighted / denominator[:, :, None]).astype(jnp.bfloat16).reshape(TILE, HEADS * HD)
        return jnp.dot(heads_out, out_weight, preferred_element_type=jnp.float32).astype(jnp.bfloat16)

    return lax.map(one_tile, jnp.arange(TILE_COUNT, dtype=jnp.int32)).reshape(NODES, OUT)
```

```python
import functools

import jax
import jax.numpy as jnp
from jax import lax
from jax.experimental import pallas as pl
from jax.experimental.pallas import tpu as pltpu
from jax.sharding import PartitionSpec as P

MESH = pl.DeviceIdType.MESH
CUT = -1e30
F32 = jnp.float32
BF16 = jnp.bfloat16
ACROSS = (((1,), (1,)), ((), ()))


def leaky_relu(values):
    return jnp.maximum(values, 0.2 * values)


def elu(values):
    low = jnp.minimum(values, 0.0)
    near = low * (1.0 + low * (0.5 + low * (1.0 / 6.0)))
    far = jnp.exp(low) - 1.0
    return jnp.where(values > 0, values, jnp.where(low > -0.015625, near, far))


def split_rows(values):
    high = values.astype(BF16).astype(F32)
    rest = values - high
    middle = rest.astype(BF16).astype(F32)
    low = rest - middle
    return jnp.concatenate([high, middle, low, jnp.zeros_like(low)], axis=0).astype(BF16)


def kernel(
    sizes,
    features,
    proj_weight,
    score_source,
    score_target,
    out_weight,
    presence,
    tile_masks,
    result,
    gathered,
    proj_buf,
    out_buf,
    mask_buf,
    cut_buf,
    vectors,
    own_proj,
    source_proj,
    partials,
    local_sem,
    outer_send,
    outer_recv,
    inner_send,
    inner_recv,
    share_send,
    share_recv,
    part_send,
    part_recv,
):
    outer, inner, heads_dev, heads, width, tile, slots = sizes
    nodes = outer * inner
    pad = vectors.shape[1]
    me = lax.axis_index("node")
    my_head = lax.axis_index("head")
    my_outer = me // inner
    my_inner = me % inner
    share = tile // heads_dev

    def outer_peer(step):
        return lax.rem(my_outer + step, outer) * inner + my_inner

    def inner_peer(step):
        return my_outer * inner + lax.rem(my_inner + step, inner)

    def head_peer(step):
        return lax.rem(my_head + step, heads_dev)

    barrier = pltpu.get_barrier_semaphore()
    for step in range(1, outer):
        pl.semaphore_signal(barrier, inc=1, device_id=(outer_peer(step), my_head), device_id_type=MESH)
    for step in range(1, inner):
        pl.semaphore_signal(barrier, inc=1, device_id=(inner_peer(step), my_head), device_id_type=MESH)
    for step in range(1, heads_dev):
        pl.semaphore_signal(barrier, inc=1, device_id=(me, head_peer(step)), device_id_type=MESH)

    def whole(node):
        return gathered.at[node]

    def part(node, head):
        return gathered.at[node, pl.ds(pl.multiple_of(head * share, share), share), :]

    load_own = pltpu.make_async_copy(features, whole(me), local_sem.at[0])
    load_proj = pltpu.make_async_copy(proj_weight, proj_buf, local_sem.at[1])
    load_mask = pltpu.make_async_copy(tile_masks.at[0], mask_buf, local_sem.at[2])
    load_out = pltpu.make_async_copy(out_weight, out_buf, local_sem.at[3])
    load_own.start()
    load_proj.start()
    load_mask.start()
    load_out.start()
    load_own.wait()
    pl.semaphore_wait(barrier, outer + inner + heads_dev - 3)

    def send(node, head, to, send_sem, recv_sem):
        copy = pltpu.make_async_remote_copy(
            src_ref=part(node, head),
            dst_ref=part(node, head),
            send_sem=send_sem,
            recv_sem=recv_sem,
            device_id=to,
            device_id_type=MESH,
        )
        copy.start()
        return copy

    def origin(hop, step):
        return lax.rem(my_outer + outer - hop, outer) * inner + lax.rem(my_inner + inner - step, inner)

    started = []

    def to_inner(hop):
        node = origin(hop, 0)
        for step in range(1, inner):
            started.append(
                send(node, my_head, (inner_peer(step), my_head), inner_send.at[hop, step], inner_recv.at[hop, step])
            )

    def to_heads(hop, step):
        node = origin(hop, step)
        for turn in range(1, heads_dev):
            started.append(
                send(
                    node,
                    my_head,
                    (me, head_peer(turn)),
                    share_send.at[hop, step, turn],
                    share_recv.at[hop, step, turn],
                )
            )

    def arrived(node, head, recv_sem):
        pltpu.make_async_copy(part(node, head), part(node, head), recv_sem).wait()

    for hop in range(1, outer):
        started.append(send(me, my_head, (outer_peer(hop), my_head), outer_send.at[hop], outer_recv.at[hop]))
    to_inner(0)

    for index, ref in enumerate((score_source, score_target)):
        vectors[index] = jnp.zeros((pad, heads * width), F32)
        for h in range(heads):
            vectors[index, h : h + 1, h * width : (h + 1) * width] = ref[h : h + 1, :]
    source_rows = split_rows(vectors[0])
    target_rows = split_rows(vectors[1])
    load_proj.wait()
    mine = jnp.dot(gathered[me], proj_buf[...], preferred_element_type=F32).astype(BF16)
    own_proj[...] = mine

    for hop in range(1, outer):
        arrived(origin(hop, 0), my_head, outer_recv.at[hop])
        to_inner(hop)
        to_heads(hop, 0)

    def own_terms(rows):
        terms = lax.dot_general(mine, rows, ACROSS, preferred_element_type=F32)
        return terms[:, 0:pad] + terms[:, pad : 2 * pad] + terms[:, 2 * pad : 3 * pad]

    target_terms = own_terms(target_rows)
    self_terms = own_terms(source_rows)

    seen = jnp.int32(0)
    ids = [jnp.int32(0)] * slots
    for j in range(nodes):
        seen = seen + presence[0, j]
        for k in range(slots):
            ids[k] = ids[k] + jnp.minimum(jnp.maximum(k + 1 - seen, 0), 1)

    load_mask.wait()
    row = lax.broadcasted_iota(jnp.int32, (tile, tile), 0)
    column = lax.broadcasted_iota(jnp.int32, (tile, tile), 1)
    diagonal = (row == column).astype(jnp.int32)
    for k in range(slots):
        own = 1 - jnp.minimum(jnp.maximum(ids[k] - me, me - ids[k]), 1)
        cut_buf[:, k * tile : (k + 1) * tile] = jnp.where(mask_buf[k] - diagonal * own == 1, 0.0, CUT)

    for hop in range(outer):
        for step in range(1, inner):
            arrived(origin(hop, step), my_head, inner_recv.at[hop, step])
            to_heads(hop, step)
    for hop in range(outer):
        for step in range(inner):
            if hop or step:
                for turn in range(1, heads_dev):
                    arrived(
                        origin(hop, step),
                        lax.rem(my_head + heads_dev - turn, heads_dev),
                        share_recv.at[hop, step, turn],
                    )

    for k in range(slots):
        source_proj[k * tile : (k + 1) * tile, :] = jnp.dot(
            gathered[jnp.minimum(ids[k], nodes - 1)], proj_buf[...], preferred_element_type=F32
        ).astype(BF16)
    terms = lax.dot_general(source_rows, source_proj[...], ACROSS, preferred_element_type=F32)
    source_terms = terms[0:pad] + terms[pad : 2 * pad] + terms[2 * pad : 3 * pad]

    heads_out = []
    for h in range(heads):
        lanes = slice(h * width, (h + 1) * width)
        target = target_terms[:, h : h + 1]
        itself = self_terms[:, h : h + 1]
        reach = source_terms[h : h + 1, :] + cut_buf[...]
        best = jnp.maximum(jnp.max(reach, axis=1, keepdims=True), itself)
        peak = leaky_relu(target + best)
        weights = jnp.exp(leaky_relu(target + reach) - peak)
        self_weight = jnp.exp(leaky_relu(target + itself) - peak)
        denominator = jnp.sum(weights, axis=1, keepdims=True) + self_weight
        total = jnp.dot(weights.astype(BF16), source_proj[:, lanes], preferred_element_type=F32)
        total = total + self_weight.astype(BF16).astype(F32) * own_proj[:, lanes].astype(F32)
        heads_out.append(elu(total / denominator).astype(BF16))
    load_out.wait()
    joined = jnp.concatenate(heads_out, axis=1)
    partials[my_head] = jnp.dot(joined, out_buf[...], preferred_element_type=F32).astype(BF16)

    for turn in range(1, heads_dev):
        copy = pltpu.make_async_remote_copy(
            src_ref=partials.at[my_head],
            dst_ref=partials.at[my_head],
            send_sem=part_send.at[turn],
            recv_sem=part_recv.at[turn],
            device_id=(me, head_peer(turn)),
            device_id_type=MESH,
        )
        copy.start()
        started.append(copy)
    for turn in range(1, heads_dev):
        source = lax.rem(my_head + heads_dev - turn, heads_dev)
        pltpu.make_async_copy(partials.at[source], partials.at[source], part_recv.at[turn]).wait()
    total = partials[0].astype(F32)
    for index in range(1, heads_dev):
        total = total + partials[index].astype(F32)
    result[...] = total.astype(BF16)
    for copy in started:
        copy.wait_send()


def per_device(nodes, heads_dev, features, proj_weight, score_source, score_target, out_weight, presence, tile_masks):
    tile = features.shape[0]
    heads, width = score_source.shape
    slots = tile_masks.shape[1]
    outputs = out_weight.shape[1]
    inner = 1
    while inner * inner * 4 <= nodes:
        inner *= 2
    outer = nodes // inner
    pad = -(-heads // 8) * 8
    sizes = (outer, inner, heads_dev, heads, width, tile, slots)
    anywhere = pl.BlockSpec(memory_space=pl.ANY)
    vmem = pl.BlockSpec(memory_space=pltpu.VMEM)
    dma = pltpu.SemaphoreType.DMA
    return pl.pallas_call(
        functools.partial(kernel, sizes),
        out_shape=jax.ShapeDtypeStruct((tile, outputs), BF16),
        in_specs=[anywhere, anywhere, vmem, vmem, anywhere, pl.BlockSpec(memory_space=pltpu.SMEM), anywhere],
        out_specs=vmem,
        scratch_shapes=[
            pltpu.VMEM((nodes, tile, features.shape[1]), BF16),
            pltpu.VMEM(proj_weight.shape, BF16),
            pltpu.VMEM(out_weight.shape, BF16),
            pltpu.VMEM(tile_masks.shape[1:], jnp.int32),
            pltpu.VMEM((tile, slots * tile), F32),
            pltpu.VMEM((2, pad, heads * width), F32),
            pltpu.VMEM((tile, heads * width), BF16),
            pltpu.VMEM((slots * tile, heads * width), BF16),
            pltpu.VMEM((heads_dev, tile, outputs), BF16),
            dma((4,)),
            dma((outer,)),
            dma((outer,)),
            dma((outer, inner)),
            dma((outer, inner)),
            dma((outer, inner, heads_dev)),
            dma((outer, inner, heads_dev)),
            dma((heads_dev,)),
            dma((heads_dev,)),
        ],
        compiler_params=pltpu.CompilerParams(
            collective_id=0, has_side_effects=True, vmem_limit_bytes=48 * 1024 * 1024
        ),
        cost_estimate=pl.CostEstimate(
            flops=2 * tile * heads * width * (features.shape[1] + outputs)
            + 2 * slots * tile * heads * width * (features.shape[1] + tile),
            bytes_accessed=4 * slots * tile * tile + 2 * nodes * tile * features.shape[1],
            transcendentals=slots * tile * tile * heads,
        ),
    )(features, proj_weight, score_source, score_target, out_weight, presence, tile_masks)


def solution(mesh):
    return jax.shard_map(
        functools.partial(per_device, mesh.shape["node"], mesh.shape["head"]),
        mesh=mesh,
        in_specs=(
            P("node", None),
            P(None, "head"),
            P("head", None),
            P("head", None),
            P("head", None),
            P("node", None),
            P("node", None, None, None),
        ),
        out_specs=P("node", None),
        check_vma=False,
    )
```

```python
import functools

import jax
import jax.numpy as jnp
from jax import lax
from jax.experimental import pallas as pl
from jax.experimental.pallas import tpu as pltpu
from jax.sharding import PartitionSpec as P

MESH = pl.DeviceIdType.MESH
CUT = -1e30
F32 = jnp.float32
BF16 = jnp.bfloat16
ACROSS = (((1,), (1,)), ((), ()))


def leaky_relu(values):
    return jnp.maximum(values, 0.2 * values)


def elu(values):
    low = jnp.minimum(values, 0.0)
    near = low * (1.0 + low * (0.5 + low * (1.0 / 6.0)))
    far = jnp.exp(low) - 1.0
    return jnp.where(values > 0, values, jnp.where(low > -0.015625, near, far))


def split_rows(values):
    high = values.astype(BF16).astype(F32)
    rest = values - high
    middle = rest.astype(BF16).astype(F32)
    low = rest - middle
    return jnp.concatenate([high, middle, low, jnp.zeros_like(low)], axis=0).astype(BF16)


def kernel(
    sizes,
    features,
    proj_weight,
    score_source,
    score_target,
    out_weight,
    presence,
    tile_masks,
    result,
    gathered,
    own_buf,
    proj_buf,
    score_buf,
    out_buf,
    presence_buf,
    mask_buf,
    cut_buf,
    vectors,
    own_proj,
    source_proj,
    partials,
    local_sem,
    outer_send,
    outer_recv,
    inner_send,
    inner_recv,
    group_send,
    group_recv,
    part_send,
    part_recv,
):
    outer, inner, heads_dev, heads, width, tile, slots = sizes
    nodes = outer * inner
    pad = vectors.shape[1]
    me = lax.axis_index("node")
    my_head = lax.axis_index("head")
    my_outer = me // inner
    my_inner = me % inner
    share = tile // heads_dev

    def outer_peer(step):
        return lax.rem(my_outer + step, outer) * inner + my_inner

    def inner_peer(step):
        return my_outer * inner + lax.rem(my_inner + step, inner)

    def head_peer(step):
        return lax.rem(my_head + step, heads_dev)

    barrier = pltpu.get_barrier_semaphore()
    for step in range(1, outer):
        pl.semaphore_signal(barrier, inc=1, device_id=(outer_peer(step), my_head), device_id_type=MESH)
    for step in range(1, inner):
        pl.semaphore_signal(barrier, inc=1, device_id=(inner_peer(step), my_head), device_id_type=MESH)
    for step in range(1, heads_dev):
        pl.semaphore_signal(barrier, inc=1, device_id=(me, head_peer(step)), device_id_type=MESH)

    own_share = features.at[pl.ds(pl.multiple_of(my_head * share, share), share), :]
    loads = []
    for source, target in (
        (features, own_buf),
        (proj_weight, proj_buf),
        (score_source, score_buf.at[0]),
        (score_target, score_buf.at[1]),
        (presence, presence_buf),
        (tile_masks.at[0], mask_buf),
        (own_share, gathered.at[my_head, me]),
        (out_weight, out_buf),
    ):
        load = pltpu.make_async_copy(source, target, local_sem.at[len(loads)])
        load.start()
        loads.append(load)
    pl.semaphore_wait(barrier, outer + inner + heads_dev - 3)

    started = []

    def send(source, target, to, send_sem, recv_sem):
        copy = pltpu.make_async_remote_copy(
            src_ref=source,
            dst_ref=target,
            send_sem=send_sem,
            recv_sem=recv_sem,
            device_id=to,
            device_id_type=MESH,
        )
        copy.start()
        started.append(copy)

    def origin_outer(hop):
        return lax.rem(my_outer + outer - hop, outer)

    def origin(hop, step):
        return origin_outer(hop) * inner + lax.rem(my_inner + inner - step, inner)

    def to_inner(hop, source):
        for step in range(1, inner):
            send(
                source,
                gathered.at[my_head, origin(hop, 0)],
                (inner_peer(step), my_head),
                inner_send.at[hop, step],
                inner_recv.at[hop, step],
            )

    def arrived(place, recv_sem):
        pltpu.make_async_copy(place, place, recv_sem).wait()

    def group(head, hop):
        return gathered.at[head, pl.ds(pl.multiple_of(origin_outer(hop) * inner, inner), inner)]

    for hop in range(1, outer):
        send(
            own_share, gathered.at[my_head, me], (outer_peer(hop), my_head), outer_send.at[hop], outer_recv.at[hop]
        )
    to_inner(0, own_share)

    for load in loads[:6]:
        load.wait()
    for index in range(2):
        vectors[index] = jnp.zeros((pad, heads * width), F32)
        for h in range(heads):
            vectors[index, h : h + 1, h * width : (h + 1) * width] = score_buf[index, h : h + 1, :]
    source_rows = split_rows(vectors[0])
    target_rows = split_rows(vectors[1])
    mine = jnp.dot(own_buf[...], proj_buf[...], preferred_element_type=F32).astype(BF16)
    own_proj[...] = mine

    def own_terms(rows):
        terms = lax.dot_general(mine, rows, ACROSS, preferred_element_type=F32)
        return terms[:, 0:pad] + terms[:, pad : 2 * pad] + terms[:, 2 * pad : 3 * pad]

    target_terms = own_terms(target_rows)
    self_terms = own_terms(source_rows)

    seen = jnp.int32(0)
    ids = [jnp.int32(0)] * slots
    for j in range(nodes):
        seen = seen + presence_buf[0, j]
        for k in range(slots):
            ids[k] = ids[k] + jnp.minimum(jnp.maximum(k + 1 - seen, 0), 1)

    row = lax.broadcasted_iota(jnp.int32, (tile, tile), 0)
    column = lax.broadcasted_iota(jnp.int32, (tile, tile), 1)
    diagonal = (row == column).astype(jnp.int32)
    for k in range(slots):
        own = 1 - jnp.minimum(jnp.maximum(ids[k] - me, me - ids[k]), 1)
        cut_buf[:, k * tile : (k + 1) * tile] = jnp.where(mask_buf[k] - diagonal * own == 1, 0.0, CUT)

    for hop in range(1, outer):
        place = gathered.at[my_head, origin(hop, 0)]
        arrived(place, outer_recv.at[hop])
        to_inner(hop, place)
    loads[6].wait()
    for hop in range(outer):
        for step in range(1, inner):
            arrived(gathered.at[my_head, origin(hop, step)], inner_recv.at[hop, step])
        for turn in range(1, heads_dev):
            send(
                group(my_head, hop),
                group(my_head, hop),
                (me, head_peer(turn)),
                group_send.at[hop, turn],
                group_recv.at[hop, turn],
            )
    for hop in range(outer):
        for turn in range(1, heads_dev):
            arrived(group(lax.rem(my_head + heads_dev - turn, heads_dev), hop), group_recv.at[hop, turn])

    for k in range(slots):
        index = jnp.minimum(ids[k], nodes - 1)
        rows = jnp.concatenate([gathered[head, index] for head in range(heads_dev)], axis=0)
        source_proj[k * tile : (k + 1) * tile, :] = jnp.dot(
            rows, proj_buf[...], preferred_element_type=F32
        ).astype(BF16)
    terms = lax.dot_general(source_rows, source_proj[...], ACROSS, preferred_element_type=F32)
    source_terms = terms[0:pad] + terms[pad : 2 * pad] + terms[2 * pad : 3 * pad]

    heads_out = []
    for h in range(heads):
        lanes = slice(h * width, (h + 1) * width)
        target = target_terms[:, h : h + 1]
        itself = self_terms[:, h : h + 1]
        reach = source_terms[h : h + 1, :] + cut_buf[...]
        best = jnp.maximum(jnp.max(reach, axis=1, keepdims=True), itself)
        peak = leaky_relu(target + best)
        weights = jnp.exp(leaky_relu(target + reach) - peak)
        self_weight = jnp.exp(leaky_relu(target + itself) - peak)
        denominator = jnp.sum(weights, axis=1, keepdims=True) + self_weight
        total = jnp.dot(weights.astype(BF16), source_proj[:, lanes], preferred_element_type=F32)
        total = total + self_weight.astype(BF16).astype(F32) * own_proj[:, lanes].astype(F32)
        heads_out.append(elu(total / denominator).astype(BF16))
    loads[7].wait()
    joined = jnp.concatenate(heads_out, axis=1)
    partials[my_head] = jnp.dot(joined, out_buf[...], preferred_element_type=F32).astype(BF16)

    for turn in range(1, heads_dev):
        send(
            partials.at[my_head], partials.at[my_head], (me, head_peer(turn)), part_send.at[turn], part_recv.at[turn]
        )
    for turn in range(1, heads_dev):
        source = lax.rem(my_head + heads_dev - turn, heads_dev)
        arrived(partials.at[source], part_recv.at[turn])
    total = partials[0].astype(F32)
    for index in range(1, heads_dev):
        total = total + partials[index].astype(F32)
    result[...] = total.astype(BF16)
    for copy in started:
        copy.wait_send()


def per_device(nodes, heads_dev, features, proj_weight, score_source, score_target, out_weight, presence, tile_masks):
    tile = features.shape[0]
    heads, width = score_source.shape
    slots = tile_masks.shape[1]
    outputs = out_weight.shape[1]
    inner = 1
    while inner * inner * 4 <= nodes:
        inner *= 2
    outer = nodes // inner
    pad = -(-heads // 8) * 8
    sizes = (outer, inner, heads_dev, heads, width, tile, slots)
    dma = pltpu.SemaphoreType.DMA
    return pl.pallas_call(
        functools.partial(kernel, sizes),
        out_shape=jax.ShapeDtypeStruct((tile, outputs), BF16),
        in_specs=[pl.BlockSpec(memory_space=pltpu.HBM)] * 7,
        out_specs=pl.BlockSpec(memory_space=pltpu.VMEM),
        scratch_shapes=[
            pltpu.VMEM((heads_dev, nodes, tile // heads_dev, features.shape[1]), BF16),
            pltpu.VMEM(features.shape, BF16),
            pltpu.VMEM(proj_weight.shape, BF16),
            pltpu.VMEM((2, heads, width), F32),
            pltpu.VMEM(out_weight.shape, BF16),
            pltpu.SMEM(presence.shape, jnp.int32),
            pltpu.VMEM(tile_masks.shape[1:], jnp.int32),
            pltpu.VMEM((tile, slots * tile), F32),
            pltpu.VMEM((2, pad, heads * width), F32),
            pltpu.VMEM((tile, heads * width), BF16),
            pltpu.VMEM((slots * tile, heads * width), BF16),
            pltpu.VMEM((heads_dev, tile, outputs), BF16),
            dma((8,)),
            dma((outer,)),
            dma((outer,)),
            dma((outer, inner)),
            dma((outer, inner)),
            dma((outer, heads_dev)),
            dma((outer, heads_dev)),
            dma((heads_dev,)),
            dma((heads_dev,)),
        ],
        compiler_params=pltpu.CompilerParams(
            collective_id=0, has_side_effects=True, vmem_limit_bytes=62 * 1024 * 1024
        ),
        cost_estimate=pl.CostEstimate(
            flops=2 * tile * heads * width * (features.shape[1] + outputs)
            + 2 * slots * tile * heads * width * (features.shape[1] + tile),
            bytes_accessed=4 * slots * tile * tile + 2 * nodes * tile * features.shape[1],
            transcendentals=slots * tile * tile * heads,
        ),
    )(features, proj_weight, score_source, score_target, out_weight, presence, tile_masks)


def solution(mesh):
    return jax.shard_map(
        functools.partial(per_device, mesh.shape["node"], mesh.shape["head"]),
        mesh=mesh,
        in_specs=(
            P("node", None),
            P(None, "head"),
            P("head", None),
            P("head", None),
            P("head", None),
            P("node", None),
            P("node", None, None, None),
        ),
        out_specs=P("node", None),
        check_vma=False,
    )
```

```python
import functools

import jax
import jax.numpy as jnp
from jax import lax
from jax.experimental import pallas as pl
from jax.experimental.pallas import tpu as pltpu
from jax.sharding import PartitionSpec as P

MESH = pl.DeviceIdType.MESH
CUT = -1e30
F32 = jnp.float32
BF16 = jnp.bfloat16
ACROSS = (((1,), (1,)), ((), ()))


def leaky_relu(values):
    return jnp.maximum(values, 0.2 * values)


def elu(values):
    low = jnp.minimum(values, 0.0)
    near = low * (1.0 + low * (0.5 + low * (1.0 / 6.0)))
    far = jnp.exp(low) - 1.0
    return jnp.where(values > 0, values, jnp.where(low > -0.015625, near, far))


def split_rows(values):
    high = values.astype(BF16).astype(F32)
    rest = values - high
    middle = rest.astype(BF16).astype(F32)
    low = rest - middle
    return jnp.concatenate([high, middle, low, jnp.zeros_like(low)], axis=0).astype(BF16)


def kernel(
    sizes,
    features,
    proj_weight,
    score_source,
    score_target,
    out_weight,
    presence,
    tile_masks,
    result,
    gathered,
    own_buf,
    proj_buf,
    score_buf,
    out_buf,
    presence_buf,
    mask_buf,
    cut_buf,
    vectors,
    own_proj,
    projected,
    source_proj,
    partials,
    local_sem,
    outer_send,
    outer_recv,
    inner_send,
    inner_recv,
    group_send,
    group_recv,
    part_send,
    part_recv,
):
    outer, inner, heads_dev, heads, width, tile, slots = sizes
    nodes = outer * inner
    pad = vectors.shape[1]
    me = lax.axis_index("node")
    my_head = lax.axis_index("head")
    my_outer = me // inner
    my_inner = me % inner
    share = tile // heads_dev

    def outer_peer(step):
        return lax.rem(my_outer + step, outer) * inner + my_inner

    def inner_peer(step):
        return my_outer * inner + lax.rem(my_inner + step, inner)

    def head_peer(step):
        return lax.rem(my_head + step, heads_dev)

    barrier = pltpu.get_barrier_semaphore()
    for step in range(1, outer):
        pl.semaphore_signal(barrier, inc=1, device_id=(outer_peer(step), my_head), device_id_type=MESH)
    for step in range(1, inner):
        pl.semaphore_signal(barrier, inc=1, device_id=(inner_peer(step), my_head), device_id_type=MESH)
    for step in range(1, heads_dev):
        pl.semaphore_signal(barrier, inc=1, device_id=(me, head_peer(step)), device_id_type=MESH)

    own_share = features.at[pl.ds(pl.multiple_of(my_head * share, share), share), :]
    loads = []
    for source, target in (
        (features, own_buf),
        (proj_weight, proj_buf),
        (score_source, score_buf.at[0]),
        (score_target, score_buf.at[1]),
        (presence, presence_buf),
        (tile_masks.at[0], mask_buf),
        (own_share, gathered.at[my_head, me]),
        (out_weight, out_buf),
    ):
        load = pltpu.make_async_copy(source, target, local_sem.at[len(loads)])
        load.start()
        loads.append(load)
    pl.semaphore_wait(barrier, outer + inner + heads_dev - 3)

    started = []

    def send(source, target, to, send_sem, recv_sem):
        copy = pltpu.make_async_remote_copy(
            src_ref=source,
            dst_ref=target,
            send_sem=send_sem,
            recv_sem=recv_sem,
            device_id=to,
            device_id_type=MESH,
        )
        copy.start()
        started.append(copy)

    def origin_outer(hop):
        return lax.rem(my_outer + outer - hop, outer)

    def origin(hop, step):
        return origin_outer(hop) * inner + lax.rem(my_inner + inner - step, inner)

    def to_inner(hop, source):
        for step in range(1, inner):
            send(
                source,
                gathered.at[my_head, origin(hop, 0)],
                (inner_peer(step), my_head),
                inner_send.at[hop, step],
                inner_recv.at[hop, step],
            )

    def arrived(place, recv_sem):
        pltpu.make_async_copy(place, place, recv_sem).wait()

    def group(head, hop):
        return gathered.at[head, pl.ds(pl.multiple_of(origin_outer(hop) * inner, inner), inner)]

    for hop in range(1, outer):
        send(
            own_share, gathered.at[my_head, me], (outer_peer(hop), my_head), outer_send.at[hop], outer_recv.at[hop]
        )
    to_inner(0, own_share)

    for load in loads[:6]:
        load.wait()
    for index in range(2):
        vectors[index] = jnp.zeros((pad, heads * width), F32)
        for h in range(heads):
            vectors[index, h : h + 1, h * width : (h + 1) * width] = score_buf[index, h : h + 1, :]
    source_rows = split_rows(vectors[0])
    target_rows = split_rows(vectors[1])
    mine = jnp.dot(own_buf[...], proj_buf[...], preferred_element_type=F32).astype(BF16)
    own_proj[...] = mine

    def own_terms(rows):
        terms = lax.dot_general(mine, rows, ACROSS, preferred_element_type=F32)
        return terms[:, 0:pad] + terms[:, pad : 2 * pad] + terms[:, 2 * pad : 3 * pad]

    target_terms = own_terms(target_rows)
    self_terms = own_terms(source_rows)

    seen = jnp.int32(0)
    ids = [jnp.int32(0)] * slots
    for j in range(nodes):
        seen = seen + presence_buf[0, j]
        for k in range(slots):
            ids[k] = ids[k] + jnp.minimum(jnp.maximum(k + 1 - seen, 0), 1)

    row = lax.broadcasted_iota(jnp.int32, (tile, tile), 0)
    column = lax.broadcasted_iota(jnp.int32, (tile, tile), 1)
    diagonal = (row == column).astype(jnp.int32)
    for k in range(slots):
        own = 1 - jnp.minimum(jnp.maximum(ids[k] - me, me - ids[k]), 1)
        cut_buf[:, k * tile : (k + 1) * tile] = jnp.where(mask_buf[k] - diagonal * own == 1, 0.0, CUT)

    for hop in range(1, outer):
        place = gathered.at[my_head, origin(hop, 0)]
        arrived(place, outer_recv.at[hop])
        to_inner(hop, place)
    loads[6].wait()

    def group_copy(hop, turn):
        return pltpu.make_async_remote_copy(
            src_ref=group(my_head, hop),
            dst_ref=group(my_head, hop),
            send_sem=group_send.at[hop, turn],
            recv_sem=group_recv.at[hop, turn],
            device_id=(me, head_peer(turn)),
            device_id_type=MESH,
        )

    def project(head, hop):
        first = pl.multiple_of(origin_outer(hop) * inner, inner)
        rows = gathered[head, pl.ds(first, inner)].reshape(inner * share, -1)
        values = jnp.dot(rows, proj_buf[...], preferred_element_type=F32).astype(BF16)
        projected[head, pl.ds(first, inner)] = values.reshape(inner, share, -1)

    def pass_on(hop, carry):
        for step in range(1, inner):
            arrived(gathered.at[my_head, origin(hop, step)], inner_recv.at[hop, step])
        for turn in range(1, heads_dev):
            group_copy(hop, turn).start()
        project(my_head, hop)
        return carry

    lax.fori_loop(0, outer, pass_on, 0)

    def take_in(hop, carry):
        for turn in range(1, heads_dev):
            head = lax.rem(my_head + heads_dev - turn, heads_dev)
            arrived(group(head, hop), group_recv.at[hop, turn])
            project(head, hop)
        return carry

    lax.fori_loop(0, outer, take_in, 0)

    for k in range(slots):
        index = jnp.minimum(ids[k], nodes - 1)
        for head in range(heads_dev):
            first = k * tile + head * share
            source_proj[first : first + share, :] = projected[head, index]
    terms = lax.dot_general(source_rows, source_proj[...], ACROSS, preferred_element_type=F32)
    source_terms = terms[0:pad] + terms[pad : 2 * pad] + terms[2 * pad : 3 * pad]

    heads_out = []
    for h in range(heads):
        lanes = slice(h * width, (h + 1) * width)
        target = jnp.broadcast_to(target_terms[:, h : h + 1], (tile, tile))
        itself = jnp.broadcast_to(self_terms[:, h : h + 1], (tile, tile))
        reach = [
            source_terms[h : h + 1, k * tile : (k + 1) * tile] + cut_buf[:, k * tile : (k + 1) * tile]
            for k in range(slots)
        ]
        best = jnp.max(functools.reduce(jnp.maximum, reach, itself), axis=1, keepdims=True)
        peak = leaky_relu(target + best)
        weights = [jnp.exp(leaky_relu(target + values) - peak) for values in reach]
        self_weight = jnp.exp(leaky_relu(target + itself) - peak)
        denominator = jnp.sum(functools.reduce(jnp.add, weights), axis=1, keepdims=True) + self_weight[:, :1]
        self_weight = self_weight[:, :1]
        rounded = jnp.concatenate([values.astype(BF16) for values in weights], axis=1)
        total = jnp.dot(rounded, source_proj[:, lanes], preferred_element_type=F32)
        total = total + self_weight.astype(BF16).astype(F32) * own_proj[:, lanes].astype(F32)
        heads_out.append(elu(total * (1.0 / denominator)).astype(BF16))
    loads[7].wait()
    joined = jnp.concatenate(heads_out, axis=1)
    partials[my_head] = jnp.dot(joined, out_buf[...], preferred_element_type=F32).astype(BF16)

    for turn in range(1, heads_dev):
        send(
            partials.at[my_head], partials.at[my_head], (me, head_peer(turn)), part_send.at[turn], part_recv.at[turn]
        )
    for turn in range(1, heads_dev):
        source = lax.rem(my_head + heads_dev - turn, heads_dev)
        arrived(partials.at[source], part_recv.at[turn])
    total = partials[0].astype(F32)
    for index in range(1, heads_dev):
        total = total + partials[index].astype(F32)
    result[...] = total.astype(BF16)
    for copy in started:
        copy.wait_send()
    for hop in range(outer):
        for turn in range(1, heads_dev):
            group_copy(hop, turn).wait_send()


def per_device(nodes, heads_dev, features, proj_weight, score_source, score_target, out_weight, presence, tile_masks):
    tile = features.shape[0]
    heads, width = score_source.shape
    slots = tile_masks.shape[1]
    outputs = out_weight.shape[1]
    inner = 1
    while inner * inner * 4 <= nodes:
        inner *= 2
    outer = nodes // inner
    pad = -(-heads // 8) * 8
    sizes = (outer, inner, heads_dev, heads, width, tile, slots)
    dma = pltpu.SemaphoreType.DMA
    return pl.pallas_call(
        functools.partial(kernel, sizes),
        out_shape=jax.ShapeDtypeStruct((tile, outputs), BF16),
        in_specs=[pl.BlockSpec(memory_space=pltpu.HBM)] * 7,
        out_specs=pl.BlockSpec(memory_space=pltpu.VMEM),
        scratch_shapes=[
            pltpu.VMEM((heads_dev, nodes, tile // heads_dev, features.shape[1]), BF16),
            pltpu.VMEM(features.shape, BF16),
            pltpu.VMEM(proj_weight.shape, BF16),
            pltpu.VMEM((2, heads, width), F32),
            pltpu.VMEM(out_weight.shape, BF16),
            pltpu.SMEM(presence.shape, jnp.int32),
            pltpu.VMEM(tile_masks.shape[1:], jnp.int32),
            pltpu.VMEM((tile, slots * tile), F32),
            pltpu.VMEM((2, pad, heads * width), F32),
            pltpu.VMEM((tile, heads * width), BF16),
            pltpu.VMEM((heads_dev, nodes, tile // heads_dev, heads * width), BF16),
            pltpu.VMEM((slots * tile, heads * width), BF16),
            pltpu.VMEM((heads_dev, tile, outputs), BF16),
            dma((8,)),
            dma((outer,)),
            dma((outer,)),
            dma((outer, inner)),
            dma((outer, inner)),
            dma((outer, heads_dev)),
            dma((outer, heads_dev)),
            dma((heads_dev,)),
            dma((heads_dev,)),
        ],
        compiler_params=pltpu.CompilerParams(
            collective_id=0, has_side_effects=True, vmem_limit_bytes=48 * 1024 * 1024
        ),
        cost_estimate=pl.CostEstimate(
            flops=2 * tile * heads * width * (features.shape[1] + outputs)
            + 2 * slots * tile * heads * width * (features.shape[1] + tile),
            bytes_accessed=4 * slots * tile * tile + 2 * nodes * tile * features.shape[1],
            transcendentals=slots * tile * tile * heads,
        ),
    )(
        *(
            pltpu.with_memory_space_constraint(operand, pltpu.HBM)
            for operand in (features, proj_weight, score_source, score_target, out_weight, presence, tile_masks)
        )
    )


def solution(mesh):
    return jax.shard_map(
        functools.partial(per_device, mesh.shape["node"], mesh.shape["head"]),
        mesh=mesh,
        in_specs=(
            P("node", None),
            P(None, "head"),
            P("head", None),
            P("head", None),
            P("head", None),
            P("node", None),
            P("node", None, None, None),
        ),
        out_specs=P("node", None),
        check_vma=False,
    )
```

```python
import functools

import jax
import jax.numpy as jnp
from jax import lax
from jax.experimental import pallas as pl
from jax.experimental.pallas import tpu as pltpu
from jax.sharding import PartitionSpec as P

MESH = pl.DeviceIdType.MESH
CUT = -1e30
F32 = jnp.float32
BF16 = jnp.bfloat16
ACROSS = (((1,), (1,)), ((), ()))


def leaky_relu(values):
    return jnp.maximum(values, 0.2 * values)


def elu(values):
    low = jnp.minimum(values, 0.0)
    near = low * (1.0 + low * (0.5 + low * (1.0 / 6.0)))
    far = jnp.exp(low) - 1.0
    return jnp.where(values > 0, values, jnp.where(low > -0.015625, near, far))


def split_rows(values):
    high = values.astype(BF16).astype(F32)
    rest = values - high
    middle = rest.astype(BF16).astype(F32)
    low = rest - middle
    return jnp.concatenate([high, middle, low, jnp.zeros_like(low)], axis=0).astype(BF16)


def kernel(
    sizes,
    features,
    proj_weight,
    score_source,
    score_target,
    out_weight,
    presence,
    tile_masks,
    result,
    gathered,
    own_buf,
    proj_buf,
    score_buf,
    out_buf,
    presence_buf,
    mask_buf,
    cut_buf,
    vectors,
    own_proj,
    projected,
    source_proj,
    partials,
    local_sem,
    outer_send,
    outer_recv,
    inner_send,
    inner_recv,
    group_send,
    group_recv,
    part_send,
    part_recv,
):
    outer, inner, heads_dev, heads, width, tile, slots = sizes
    nodes = outer * inner
    pad = vectors.shape[1]
    me = lax.axis_index("node")
    my_head = lax.axis_index("head")
    my_outer = me // inner
    my_inner = me % inner
    share = tile // heads_dev

    def paired(position, step, size):
        other = 0
        bit = 1
        while bit < size:
            other = other + bit * ((position // bit + step // bit) % 2)
            bit *= 2
        return other

    def outer_peer(step):
        return paired(my_outer, step, outer) * inner + my_inner

    def inner_peer(step):
        return my_outer * inner + paired(my_inner, step, inner)

    def head_peer(step):
        return lax.rem(my_head + step, heads_dev)

    barrier = pltpu.get_barrier_semaphore()
    for step in range(1, outer):
        pl.semaphore_signal(barrier, inc=1, device_id=(outer_peer(step), my_head), device_id_type=MESH)
    for step in range(1, inner):
        pl.semaphore_signal(barrier, inc=1, device_id=(inner_peer(step), my_head), device_id_type=MESH)
    for step in range(1, heads_dev):
        pl.semaphore_signal(barrier, inc=1, device_id=(me, head_peer(step)), device_id_type=MESH)

    own_share = features.at[pl.ds(pl.multiple_of(my_head * share, share), share), :]
    pl.semaphore_wait(barrier, outer + inner + heads_dev - 3)

    started = []

    def send(source, target, to, send_sem, recv_sem):
        copy = pltpu.make_async_remote_copy(
            src_ref=source,
            dst_ref=target,
            send_sem=send_sem,
            recv_sem=recv_sem,
            device_id=to,
            device_id_type=MESH,
        )
        copy.start()
        started.append(copy)

    def origin_outer(hop):
        return paired(my_outer, hop, outer)

    def origin(hop, step):
        return origin_outer(hop) * inner + paired(my_inner, step, inner)

    def to_inner(hop, source):
        for step in reversed(range(1, inner)):
            send(
                source,
                gathered.at[my_head, origin(hop, 0)],
                (inner_peer(step), my_head),
                inner_send.at[hop, step],
                inner_recv.at[hop, step],
            )

    def arrived(place, recv_sem):
        pltpu.make_async_copy(place, place, recv_sem).wait()

    def group(head, hop):
        return gathered.at[head, pl.ds(pl.multiple_of(origin_outer(hop) * inner, inner), inner)]

    for hop in range(1, outer):
        send(
            own_share, gathered.at[my_head, me], (outer_peer(hop), my_head), outer_send.at[hop], outer_recv.at[hop]
        )
    to_inner(0, own_share)

    loads = []
    for source, target in (
        (features, own_buf),
        (proj_weight, proj_buf),
        (score_source, score_buf.at[0]),
        (score_target, score_buf.at[1]),
        (presence, presence_buf),
        (tile_masks.at[0], mask_buf),
        (own_share, gathered.at[my_head, me]),
        (out_weight, out_buf),
    ):
        load = pltpu.make_async_copy(source, target, local_sem.at[len(loads)])
        load.start()
        loads.append(load)

    for hop in range(1, outer):
        place = gathered.at[my_head, origin(hop, 0)]
        arrived(place, outer_recv.at[hop])
        to_inner(hop, place)

    for load in loads[:6]:
        load.wait()
    for index in range(2):
        vectors[index] = jnp.zeros((pad, heads * width), F32)
        for h in range(heads):
            vectors[index, h : h + 1, h * width : (h + 1) * width] = score_buf[index, h : h + 1, :]
    source_rows = split_rows(vectors[0])
    target_rows = split_rows(vectors[1])
    mine = jnp.dot(own_buf[...], proj_buf[...], preferred_element_type=F32).astype(BF16)
    own_proj[...] = mine

    def own_terms(rows):
        terms = lax.dot_general(mine, rows, ACROSS, preferred_element_type=F32)
        return terms[:, 0:pad] + terms[:, pad : 2 * pad] + terms[:, 2 * pad : 3 * pad]

    target_terms = own_terms(target_rows)
    self_terms = own_terms(source_rows)

    seen = jnp.int32(0)
    ids = [jnp.int32(0)] * slots
    for j in range(nodes):
        seen = seen + presence_buf[0, j]
        for k in range(slots):
            ids[k] = ids[k] + jnp.minimum(jnp.maximum(k + 1 - seen, 0), 1)

    row = lax.broadcasted_iota(jnp.int32, (tile, tile), 0)
    column = lax.broadcasted_iota(jnp.int32, (tile, tile), 1)
    diagonal = (row == column).astype(jnp.int32)
    for k in range(slots):
        own = 1 - jnp.minimum(jnp.maximum(ids[k] - me, me - ids[k]), 1)
        cut_buf[:, k * tile : (k + 1) * tile] = jnp.where(mask_buf[k] - diagonal * own == 1, 0.0, CUT)

    loads[6].wait()

    def group_copy(hop, turn):
        return pltpu.make_async_remote_copy(
            src_ref=group(my_head, hop),
            dst_ref=group(my_head, hop),
            send_sem=group_send.at[hop, turn],
            recv_sem=group_recv.at[hop, turn],
            device_id=(me, head_peer(turn)),
            device_id_type=MESH,
        )

    def project(head, hop):
        first = pl.multiple_of(origin_outer(hop) * inner, inner)
        rows = gathered[head, pl.ds(first, inner)].reshape(inner * share, -1)
        values = jnp.dot(rows, proj_buf[...], preferred_element_type=F32).astype(BF16)
        projected[head, pl.ds(first, inner)] = values.reshape(inner, share, -1)

    def pass_on(hop, carry):
        for step in range(1, inner):
            arrived(gathered.at[my_head, origin(hop, step)], inner_recv.at[hop, step])
        for turn in range(1, heads_dev):
            group_copy(hop, turn).start()
        project(my_head, hop)
        return carry

    lax.fori_loop(0, outer, pass_on, 0)

    def take_in(hop, carry):
        for turn in range(1, heads_dev):
            head = lax.rem(my_head + heads_dev - turn, heads_dev)
            arrived(group(head, hop), group_recv.at[hop, turn])
            project(head, hop)
        return carry

    lax.fori_loop(0, outer, take_in, 0)

    for k in range(slots):
        index = jnp.minimum(ids[k], nodes - 1)
        for head in range(heads_dev):
            first = k * tile + head * share
            source_proj[first : first + share, :] = projected[head, index]
    terms = lax.dot_general(source_rows, source_proj[...], ACROSS, preferred_element_type=F32)
    source_terms = terms[0:pad] + terms[pad : 2 * pad] + terms[2 * pad : 3 * pad]

    heads_out = []
    for h in range(heads):
        lanes = slice(h * width, (h + 1) * width)
        target = jnp.broadcast_to(target_terms[:, h : h + 1], (tile, tile))
        itself = jnp.broadcast_to(self_terms[:, h : h + 1], (tile, tile))
        reach = [
            source_terms[h : h + 1, k * tile : (k + 1) * tile] + cut_buf[:, k * tile : (k + 1) * tile]
            for k in range(slots)
        ]
        best = jnp.max(functools.reduce(jnp.maximum, reach, itself), axis=1, keepdims=True)
        peak = leaky_relu(target + best)
        weights = [jnp.exp(leaky_relu(target + values) - peak) for values in reach]
        self_weight = jnp.exp(leaky_relu(target + itself) - peak)
        denominator = jnp.sum(functools.reduce(jnp.add, weights), axis=1, keepdims=True) + self_weight[:, :1]
        self_weight = self_weight[:, :1]
        rounded = jnp.concatenate([values.astype(BF16) for values in weights], axis=1)
        total = jnp.dot(rounded, source_proj[:, lanes], preferred_element_type=F32)
        total = total + self_weight.astype(BF16).astype(F32) * own_proj[:, lanes].astype(F32)
        heads_out.append(elu(total * (1.0 / denominator)).astype(BF16))
    loads[7].wait()
    joined = jnp.concatenate(heads_out, axis=1)
    partials[my_head] = jnp.dot(joined, out_buf[...], preferred_element_type=F32).astype(BF16)

    for turn in range(1, heads_dev):
        send(
            partials.at[my_head], partials.at[my_head], (me, head_peer(turn)), part_send.at[turn], part_recv.at[turn]
        )
    for turn in range(1, heads_dev):
        source = lax.rem(my_head + heads_dev - turn, heads_dev)
        arrived(partials.at[source], part_recv.at[turn])
    total = partials[0].astype(F32)
    for index in range(1, heads_dev):
        total = total + partials[index].astype(F32)
    result[...] = total.astype(BF16)
    for copy in started:
        copy.wait_send()
    for hop in range(outer):
        for turn in range(1, heads_dev):
            group_copy(hop, turn).wait_send()


def per_device(nodes, heads_dev, features, proj_weight, score_source, score_target, out_weight, presence, tile_masks):
    tile = features.shape[0]
    heads, width = score_source.shape
    slots = tile_masks.shape[1]
    outputs = out_weight.shape[1]
    inner = 1
    while inner * inner * 4 <= nodes:
        inner *= 2
    outer = nodes // inner
    assert outer & (outer - 1) == 0
    pad = -(-heads // 8) * 8
    sizes = (outer, inner, heads_dev, heads, width, tile, slots)
    dma = pltpu.SemaphoreType.DMA
    return pl.pallas_call(
        functools.partial(kernel, sizes),
        out_shape=jax.ShapeDtypeStruct((tile, outputs), BF16),
        in_specs=[pl.BlockSpec(memory_space=pltpu.HBM)] * 7,
        out_specs=pl.BlockSpec(memory_space=pltpu.VMEM),
        scratch_shapes=[
            pltpu.VMEM((heads_dev, nodes, tile // heads_dev, features.shape[1]), BF16),
            pltpu.VMEM(features.shape, BF16),
            pltpu.VMEM(proj_weight.shape, BF16),
            pltpu.VMEM((2, heads, width), F32),
            pltpu.VMEM(out_weight.shape, BF16),
            pltpu.SMEM(presence.shape, jnp.int32),
            pltpu.VMEM(tile_masks.shape[1:], jnp.int32),
            pltpu.VMEM((tile, slots * tile), F32),
            pltpu.VMEM((2, pad, heads * width), F32),
            pltpu.VMEM((tile, heads * width), BF16),
            pltpu.VMEM((heads_dev, nodes, tile // heads_dev, heads * width), BF16),
            pltpu.VMEM((slots * tile, heads * width), BF16),
            pltpu.VMEM((heads_dev, tile, outputs), BF16),
            dma((8,)),
            dma((outer,)),
            dma((outer,)),
            dma((outer, inner)),
            dma((outer, inner)),
            dma((outer, heads_dev)),
            dma((outer, heads_dev)),
            dma((heads_dev,)),
            dma((heads_dev,)),
        ],
        compiler_params=pltpu.CompilerParams(
            collective_id=0, has_side_effects=True, vmem_limit_bytes=48 * 1024 * 1024
        ),
        cost_estimate=pl.CostEstimate(
            flops=2 * tile * heads * width * (features.shape[1] + outputs)
            + 2 * slots * tile * heads * width * (features.shape[1] + tile),
            bytes_accessed=4 * slots * tile * tile + 2 * nodes * tile * features.shape[1],
            transcendentals=slots * tile * tile * heads,
        ),
    )(
        *(
            pltpu.with_memory_space_constraint(operand, pltpu.HBM)
            for operand in (features, proj_weight, score_source, score_target, out_weight, presence, tile_masks)
        )
    )


def solution(mesh):
    return jax.shard_map(
        functools.partial(per_device, mesh.shape["node"], mesh.shape["head"]),
        mesh=mesh,
        in_specs=(
            P("node", None),
            P(None, "head"),
            P("head", None),
            P("head", None),
            P("head", None),
            P("node", None),
            P("node", None, None, None),
        ),
        out_specs=P("node", None),
        check_vma=False,
    )
```

```python
import functools

import jax
import jax.numpy as jnp
from jax import lax
from jax.experimental import pallas as pl
from jax.experimental.pallas import tpu as pltpu
from jax.sharding import PartitionSpec as P

MESH = pl.DeviceIdType.MESH
CUT = -1e30
F32 = jnp.float32
BF16 = jnp.bfloat16
ACROSS = (((1,), (1,)), ((), ()))


def leaky_relu(values):
    return jnp.maximum(values, 0.2 * values)


def elu(values):
    low = jnp.minimum(values, 0.0)
    near = low * (1.0 + low * (0.5 + low * (1.0 / 6.0)))
    far = jnp.exp(low) - 1.0
    return jnp.where(values > 0, values, jnp.where(low > -0.015625, near, far))


def split_rows(values):
    high = values.astype(BF16).astype(F32)
    rest = values - high
    middle = rest.astype(BF16).astype(F32)
    low = rest - middle
    return jnp.concatenate([high, middle, low, jnp.zeros_like(low)], axis=0).astype(BF16)


def kernel(
    sizes,
    features,
    proj_weight,
    score_source,
    score_target,
    out_weight,
    presence,
    tile_masks,
    result,
    gathered,
    own_buf,
    proj_buf,
    score_buf,
    out_buf,
    presence_buf,
    mask_buf,
    cut_buf,
    vectors,
    own_proj,
    projected,
    source_proj,
    spread,
    source_terms,
    rounded,
    scales,
    partials,
    local_sem,
    outer_send,
    outer_recv,
    inner_send,
    inner_recv,
    group_send,
    group_recv,
    part_send,
    part_recv,
):
    outer, inner, heads_dev, heads, width, tile, slots = sizes
    nodes = outer * inner
    pad = vectors.shape[1]
    me = lax.axis_index("node")
    my_head = lax.axis_index("head")
    my_outer = me // inner
    my_inner = me % inner
    share = tile // heads_dev
    chunk = min(tile, 32)

    def paired(position, step, size):
        other = 0
        bit = 1
        while bit < size:
            other = other + bit * ((position // bit + step // bit) % 2)
            bit *= 2
        return other

    def outer_peer(step):
        return paired(my_outer, step, outer) * inner + my_inner

    def inner_peer(step):
        return my_outer * inner + paired(my_inner, step, inner)

    def head_peer(step):
        return lax.rem(my_head + step, heads_dev)

    barrier = pltpu.get_barrier_semaphore()
    for step in range(1, outer):
        pl.semaphore_signal(barrier, inc=1, device_id=(outer_peer(step), my_head), device_id_type=MESH)
    for step in range(1, inner):
        pl.semaphore_signal(barrier, inc=1, device_id=(inner_peer(step), my_head), device_id_type=MESH)
    for step in range(1, heads_dev):
        pl.semaphore_signal(barrier, inc=1, device_id=(me, head_peer(step)), device_id_type=MESH)

    own_share = features.at[pl.ds(pl.multiple_of(my_head * share, share), share), :]
    pl.semaphore_wait(barrier, outer + inner + heads_dev - 3)

    started = []

    def send(source, target, to, send_sem, recv_sem):
        copy = pltpu.make_async_remote_copy(
            src_ref=source,
            dst_ref=target,
            send_sem=send_sem,
            recv_sem=recv_sem,
            device_id=to,
            device_id_type=MESH,
        )
        copy.start()
        started.append(copy)

    def origin_outer(hop):
        return paired(my_outer, hop, outer)

    def origin(hop, step):
        return origin_outer(hop) * inner + paired(my_inner, step, inner)

    def to_inner(hop, source):
        for step in reversed(range(1, inner)):
            send(
                source,
                gathered.at[my_head, origin(hop, 0)],
                (inner_peer(step), my_head),
                inner_send.at[hop, step],
                inner_recv.at[hop, step],
            )

    def arrived(place, recv_sem):
        pltpu.make_async_copy(place, place, recv_sem).wait()

    def group(head, hop):
        return gathered.at[head, pl.ds(pl.multiple_of(origin_outer(hop) * inner, inner), inner)]

    for hop in range(1, outer):
        send(
            own_share, gathered.at[my_head, me], (outer_peer(hop), my_head), outer_send.at[hop], outer_recv.at[hop]
        )
    to_inner(0, own_share)

    loads = []
    for source, target in (
        (features, own_buf),
        (proj_weight, proj_buf),
        (score_source, score_buf.at[0]),
        (score_target, score_buf.at[1]),
        (presence, presence_buf),
        (tile_masks.at[0], mask_buf),
        (own_share, gathered.at[my_head, me]),
        (out_weight, out_buf),
    ):
        load = pltpu.make_async_copy(source, target, local_sem.at[len(loads)])
        load.start()
        loads.append(load)

    for hop in range(1, outer):
        place = gathered.at[my_head, origin(hop, 0)]
        arrived(place, outer_recv.at[hop])
        to_inner(hop, place)

    for load in loads[:6]:
        load.wait()
    for index in range(2):
        vectors[index] = jnp.zeros((pad, heads * width), F32)
        for h in range(heads):
            vectors[index, h : h + 1, h * width : (h + 1) * width] = score_buf[index, h : h + 1, :]
    source_rows = split_rows(vectors[0])
    target_rows = split_rows(vectors[1])
    mine = jnp.dot(own_buf[...], proj_buf[...], preferred_element_type=F32).astype(BF16)
    own_proj[...] = mine

    def own_terms(rows):
        terms = lax.dot_general(mine, rows, ACROSS, preferred_element_type=F32)
        return terms[:, 0:pad] + terms[:, pad : 2 * pad] + terms[:, 2 * pad : 3 * pad]

    for index, rows in enumerate((target_rows, source_rows)):
        terms = own_terms(rows)
        for h in range(heads):
            spread[index, h] = jnp.broadcast_to(terms[:, h : h + 1], (tile, tile))

    seen = jnp.int32(0)
    ids = [jnp.int32(0)] * slots
    for j in range(nodes):
        seen = seen + presence_buf[0, j]
        for k in range(slots):
            ids[k] = ids[k] + jnp.minimum(jnp.maximum(k + 1 - seen, 0), 1)

    row = lax.broadcasted_iota(jnp.int32, (tile, tile), 0)
    column = lax.broadcasted_iota(jnp.int32, (tile, tile), 1)
    diagonal = (row == column).astype(jnp.int32)
    for k in range(slots):
        own = 1 - jnp.minimum(jnp.maximum(ids[k] - me, me - ids[k]), 1)
        cut_buf[:, k * tile : (k + 1) * tile] = jnp.where(mask_buf[k] - diagonal * own == 1, 0.0, CUT)

    loads[6].wait()

    def group_copy(hop, turn):
        return pltpu.make_async_remote_copy(
            src_ref=group(my_head, hop),
            dst_ref=group(my_head, hop),
            send_sem=group_send.at[hop, turn],
            recv_sem=group_recv.at[hop, turn],
            device_id=(me, head_peer(turn)),
            device_id_type=MESH,
        )

    def project(head, hop):
        first = pl.multiple_of(origin_outer(hop) * inner, inner)
        rows = gathered[head, pl.ds(first, inner)].reshape(inner * share, -1)
        values = jnp.dot(rows, proj_buf[...], preferred_element_type=F32).astype(BF16)
        projected[head, pl.ds(first, inner)] = values.reshape(inner, share, -1)

    def pass_on(hop, carry):
        for step in range(1, inner):
            arrived(gathered.at[my_head, origin(hop, step)], inner_recv.at[hop, step])
        for turn in range(1, heads_dev):
            group_copy(hop, turn).start()
        project(my_head, hop)
        return carry

    lax.fori_loop(0, outer, pass_on, 0)

    def take_in(hop, carry):
        for turn in range(1, heads_dev):
            head = lax.rem(my_head + heads_dev - turn, heads_dev)
            arrived(group(head, hop), group_recv.at[hop, turn])
            project(head, hop)
        return carry

    lax.fori_loop(0, outer, take_in, 0)

    for k in range(slots):
        index = jnp.minimum(ids[k], nodes - 1)
        for head in range(heads_dev):
            first = k * tile + head * share
            source_proj[first : first + share, :] = projected[head, index]
    terms = lax.dot_general(source_rows, source_proj[...], ACROSS, preferred_element_type=F32)
    source_terms[...] = terms[0:pad] + terms[pad : 2 * pad] + terms[2 * pad : 3 * pad]

    def weigh(index, carry):
        lines = pl.ds(pl.multiple_of(index * chunk, chunk), chunk)
        for h in range(heads):
            target = spread[0, h, lines, :]
            itself = spread[1, h, lines, :]
            reach = [
                source_terms[h : h + 1, k * tile : (k + 1) * tile] + cut_buf[lines, k * tile : (k + 1) * tile]
                for k in range(slots)
            ]
            best = jnp.max(functools.reduce(jnp.maximum, reach, itself), axis=1, keepdims=True)
            peak = leaky_relu(target + best)
            weights = [jnp.exp(leaky_relu(target + values) - peak) for values in reach]
            self_weight = jnp.exp(leaky_relu(target + itself) - peak)
            denominator = jnp.sum(functools.reduce(jnp.add, weights), axis=1, keepdims=True) + self_weight
            for k in range(slots):
                rounded[h, lines, k * tile : (k + 1) * tile] = weights[k].astype(BF16)
            scales[0, h, lines, :] = 1.0 / denominator
            scales[1, h, lines, :] = self_weight
        return carry

    lax.fori_loop(0, tile // chunk, weigh, 0)

    heads_out = []
    for h in range(heads):
        lanes = slice(h * width, (h + 1) * width)
        total = jnp.dot(rounded[h], source_proj[:, lanes], preferred_element_type=F32)
        self_weight = scales[1, h][:, :width].astype(BF16).astype(F32)
        total = total + self_weight * own_proj[:, lanes].astype(F32)
        heads_out.append(elu(total * scales[0, h][:, :width]).astype(BF16))
    loads[7].wait()
    joined = jnp.concatenate(heads_out, axis=1)
    partials[my_head] = jnp.dot(joined, out_buf[...], preferred_element_type=F32).astype(BF16)

    for turn in range(1, heads_dev):
        send(
            partials.at[my_head], partials.at[my_head], (me, head_peer(turn)), part_send.at[turn], part_recv.at[turn]
        )
    for turn in range(1, heads_dev):
        source = lax.rem(my_head + heads_dev - turn, heads_dev)
        arrived(partials.at[source], part_recv.at[turn])
    total = partials[0].astype(F32)
    for index in range(1, heads_dev):
        total = total + partials[index].astype(F32)
    result[...] = total.astype(BF16)
    for copy in started:
        copy.wait_send()
    for hop in range(outer):
        for turn in range(1, heads_dev):
            group_copy(hop, turn).wait_send()


def per_device(nodes, heads_dev, features, proj_weight, score_source, score_target, out_weight, presence, tile_masks):
    tile = features.shape[0]
    heads, width = score_source.shape
    slots = tile_masks.shape[1]
    outputs = out_weight.shape[1]
    inner = 1
    while inner * inner * 4 <= nodes:
        inner *= 2
    outer = nodes // inner
    assert width <= tile
    assert outer & (outer - 1) == 0
    pad = -(-heads // 8) * 8
    sizes = (outer, inner, heads_dev, heads, width, tile, slots)
    dma = pltpu.SemaphoreType.DMA
    return pl.pallas_call(
        functools.partial(kernel, sizes),
        out_shape=jax.ShapeDtypeStruct((tile, outputs), BF16),
        in_specs=[pl.BlockSpec(memory_space=pltpu.HBM)] * 7,
        out_specs=pl.BlockSpec(memory_space=pltpu.VMEM),
        scratch_shapes=[
            pltpu.VMEM((heads_dev, nodes, tile // heads_dev, features.shape[1]), BF16),
            pltpu.VMEM(features.shape, BF16),
            pltpu.VMEM(proj_weight.shape, BF16),
            pltpu.VMEM((2, heads, width), F32),
            pltpu.VMEM(out_weight.shape, BF16),
            pltpu.SMEM(presence.shape, jnp.int32),
            pltpu.VMEM(tile_masks.shape[1:], jnp.int32),
            pltpu.VMEM((tile, slots * tile), F32),
            pltpu.VMEM((2, pad, heads * width), F32),
            pltpu.VMEM((tile, heads * width), BF16),
            pltpu.VMEM((heads_dev, nodes, tile // heads_dev, heads * width), BF16),
            pltpu.VMEM((slots * tile, heads * width), BF16),
            pltpu.VMEM((2, heads, tile, tile), F32),
            pltpu.VMEM((pad, slots * tile), F32),
            pltpu.VMEM((heads, tile, slots * tile), BF16),
            pltpu.VMEM((2, heads, tile, tile), F32),
            pltpu.VMEM((heads_dev, tile, outputs), BF16),
            dma((8,)),
            dma((outer,)),
            dma((outer,)),
            dma((outer, inner)),
            dma((outer, inner)),
            dma((outer, heads_dev)),
            dma((outer, heads_dev)),
            dma((heads_dev,)),
            dma((heads_dev,)),
        ],
        compiler_params=pltpu.CompilerParams(
            collective_id=0, has_side_effects=True, vmem_limit_bytes=48 * 1024 * 1024
        ),
        cost_estimate=pl.CostEstimate(
            flops=2 * tile * heads * width * (features.shape[1] + outputs)
            + 2 * slots * tile * heads * width * (features.shape[1] + tile),
            bytes_accessed=4 * slots * tile * tile + 2 * nodes * tile * features.shape[1],
            transcendentals=slots * tile * tile * heads,
        ),
    )(
        *(
            pltpu.with_memory_space_constraint(operand, pltpu.HBM)
            for operand in (features, proj_weight, score_source, score_target, out_weight, presence, tile_masks)
        )
    )


def solution(mesh):
    return jax.shard_map(
        functools.partial(per_device, mesh.shape["node"], mesh.shape["head"]),
        mesh=mesh,
        in_specs=(
            P("node", None),
            P(None, "head"),
            P("head", None),
            P("head", None),
            P("head", None),
            P("node", None),
            P("node", None, None, None),
        ),
        out_specs=P("node", None),
        check_vma=False,
    )
```

```python
import functools

import jax
import jax.numpy as jnp
from jax import lax
from jax.experimental import pallas as pl
from jax.experimental.pallas import tpu as pltpu
from jax.sharding import PartitionSpec as P

MESH = pl.DeviceIdType.MESH
CUT = -1e30
F32 = jnp.float32
BF16 = jnp.bfloat16
ACROSS = (((1,), (1,)), ((), ()))


def leaky_relu(values):
    return jnp.maximum(values, 0.2 * values)


def elu(values):
    low = jnp.minimum(values, 0.0)
    near = low * (1.0 + low * (0.5 + low * (1.0 / 6.0)))
    far = jnp.exp(low) - 1.0
    return jnp.where(values > 0, values, jnp.where(low > -0.015625, near, far))


def split_rows(values):
    high = values.astype(BF16).astype(F32)
    rest = values - high
    middle = rest.astype(BF16).astype(F32)
    low = rest - middle
    return jnp.concatenate([high, middle, low, jnp.zeros_like(low)], axis=0).astype(BF16)


def kernel(
    sizes,
    features,
    proj_weight,
    score_source,
    score_target,
    out_weight,
    presence,
    tile_masks,
    result,
    gathered,
    others,
    own_buf,
    proj_buf,
    score_buf,
    out_buf,
    presence_buf,
    mask_buf,
    cut_buf,
    vectors,
    own_proj,
    source_proj,
    partials,
    local_sem,
    outer_send,
    outer_recv,
    inner_send,
    inner_recv,
    group_send,
    group_recv,
    part_send,
    part_recv,
):
    outer, inner, heads_dev, heads, width, tile, slots = sizes
    nodes = outer * inner
    pad = vectors.shape[1]
    me = lax.axis_index("node")
    my_head = lax.axis_index("head")
    my_outer = me // inner
    my_inner = me % inner
    share = tile // heads_dev

    def paired(position, step, size):
        other = 0
        bit = 1
        while bit < size:
            other = other + bit * ((position // bit + step // bit) % 2)
            bit *= 2
        return other

    def outer_peer(step):
        return paired(my_outer, step, outer) * inner + my_inner

    def inner_peer(step):
        return my_outer * inner + paired(my_inner, step, inner)

    def head_peer(step):
        return lax.rem(my_head + step, heads_dev)

    barrier = pltpu.get_barrier_semaphore()
    for step in range(1, outer):
        pl.semaphore_signal(barrier, inc=1, device_id=(outer_peer(step), my_head), device_id_type=MESH)
    for step in range(1, inner):
        pl.semaphore_signal(barrier, inc=1, device_id=(inner_peer(step), my_head), device_id_type=MESH)
    for step in range(1, heads_dev):
        pl.semaphore_signal(barrier, inc=1, device_id=(me, head_peer(step)), device_id_type=MESH)

    own_share = features.at[pl.ds(pl.multiple_of(my_head * share, share), share), :]
    pl.semaphore_wait(barrier, outer + inner + heads_dev - 3)

    started = []

    def send(source, target, to, send_sem, recv_sem):
        copy = pltpu.make_async_remote_copy(
            src_ref=source,
            dst_ref=target,
            send_sem=send_sem,
            recv_sem=recv_sem,
            device_id=to,
            device_id_type=MESH,
        )
        copy.start()
        started.append(copy)

    def origin_outer(hop):
        return paired(my_outer, hop, outer)

    def origin(hop, step):
        return origin_outer(hop) * inner + paired(my_inner, step, inner)

    def to_inner(hop, source):
        for step in reversed(range(1, inner)):
            send(
                source,
                gathered.at[origin(hop, 0)],
                (inner_peer(step), my_head),
                inner_send.at[hop, step],
                inner_recv.at[hop, step],
            )

    def arrived(place, recv_sem):
        pltpu.make_async_copy(place, place, recv_sem).wait()

    def group(place, hop):
        return place.at[pl.ds(pl.multiple_of(origin_outer(hop) * inner, inner), inner)]

    for hop in range(1, outer):
        send(
            own_share, gathered.at[me], (outer_peer(hop), my_head), outer_send.at[hop], outer_recv.at[hop]
        )
    to_inner(0, own_share)

    loads = []
    for source, target in (
        (features, own_buf),
        (proj_weight, proj_buf),
        (score_source, score_buf.at[0]),
        (score_target, score_buf.at[1]),
        (presence, presence_buf),
        (tile_masks.at[0], mask_buf),
        (own_share, gathered.at[me]),
        (out_weight, out_buf),
    ):
        load = pltpu.make_async_copy(source, target, local_sem.at[len(loads)])
        load.start()
        loads.append(load)

    for hop in range(1, outer):
        place = gathered.at[origin(hop, 0)]
        arrived(place, outer_recv.at[hop])
        to_inner(hop, place)

    for load in loads[:6]:
        load.wait()
    for index in range(2):
        vectors[index] = jnp.zeros((pad, heads * width), F32)
        for h in range(heads):
            vectors[index, h : h + 1, h * width : (h + 1) * width] = score_buf[index, h : h + 1, :]
    source_rows = split_rows(vectors[0])
    target_rows = split_rows(vectors[1])
    mine = jnp.dot(own_buf[...], proj_buf[...], preferred_element_type=F32).astype(BF16)
    own_proj[...] = mine

    def own_terms(rows):
        terms = lax.dot_general(mine, rows, ACROSS, preferred_element_type=F32)
        return terms[:, 0:pad] + terms[:, pad : 2 * pad] + terms[:, 2 * pad : 3 * pad]

    target_terms = own_terms(target_rows)
    self_terms = own_terms(source_rows)

    seen = jnp.int32(0)
    ids = [jnp.int32(0)] * slots
    for j in range(nodes):
        seen = seen + presence_buf[0, j]
        for k in range(slots):
            ids[k] = ids[k] + jnp.minimum(jnp.maximum(k + 1 - seen, 0), 1)

    row = lax.broadcasted_iota(jnp.int32, (tile, tile), 0)
    column = lax.broadcasted_iota(jnp.int32, (tile, tile), 1)
    diagonal = (row == column).astype(jnp.int32)
    for k in range(slots):
        own = 1 - jnp.minimum(jnp.maximum(ids[k] - me, me - ids[k]), 1)
        cut_buf[:, k * tile : (k + 1) * tile] = jnp.where(mask_buf[k] - diagonal * own == 1, 0.0, CUT)

    loads[6].wait()

    def group_copy(hop, turn):
        return pltpu.make_async_remote_copy(
            src_ref=group(gathered, hop),
            dst_ref=group(others.at[turn - 1], hop),
            send_sem=group_send.at[hop, turn],
            recv_sem=group_recv.at[hop, turn],
            device_id=(me, head_peer(turn)),
            device_id_type=MESH,
        )

    def project(place, head):
        rows = [place[jnp.minimum(ids[k], nodes - 1)] for k in range(slots)]
        values = jnp.dot(
            jnp.concatenate(rows, axis=0), proj_buf[...], preferred_element_type=F32
        ).astype(BF16)
        for k in range(slots):
            first = pl.multiple_of(k * tile + head * share, share)
            source_proj[pl.ds(first, share), :] = values[k * share : (k + 1) * share]

    for hop in range(outer):
        for step in range(1, inner):
            arrived(gathered.at[origin(hop, step)], inner_recv.at[hop, step])
        for turn in range(1, heads_dev):
            group_copy(hop, turn).start()
    project(gathered, my_head)
    for hop in range(outer):
        for turn in range(1, heads_dev):
            arrived(group(others.at[turn - 1], hop), group_recv.at[hop, turn])
    for turn in range(1, heads_dev):
        project(others.at[turn - 1], lax.rem(my_head + heads_dev - turn, heads_dev))
    terms = lax.dot_general(source_rows, source_proj[...], ACROSS, preferred_element_type=F32)
    source_terms = terms[0:pad] + terms[pad : 2 * pad] + terms[2 * pad : 3 * pad]

    heads_out = []
    for h in range(heads):
        lanes = slice(h * width, (h + 1) * width)
        target = jnp.broadcast_to(target_terms[:, h : h + 1], (tile, tile))
        itself = jnp.broadcast_to(self_terms[:, h : h + 1], (tile, tile))
        reach = [
            source_terms[h : h + 1, k * tile : (k + 1) * tile] + cut_buf[:, k * tile : (k + 1) * tile]
            for k in range(slots)
        ]
        best = jnp.max(functools.reduce(jnp.maximum, reach, itself), axis=1, keepdims=True)
        peak = leaky_relu(target + best)
        weights = [jnp.exp(leaky_relu(target + values) - peak) for values in reach]
        self_weight = jnp.exp(leaky_relu(target + itself) - peak)
        denominator = jnp.sum(functools.reduce(jnp.add, weights), axis=1, keepdims=True) + self_weight[:, :1]
        self_weight = self_weight[:, :1]
        rounded = jnp.concatenate([values.astype(BF16) for values in weights], axis=1)
        total = jnp.dot(rounded, source_proj[:, lanes], preferred_element_type=F32)
        total = total + self_weight.astype(BF16).astype(F32) * own_proj[:, lanes].astype(F32)
        heads_out.append(elu(total * (1.0 / denominator)).astype(BF16))
    loads[7].wait()
    joined = jnp.concatenate(heads_out, axis=1)
    partials[my_head] = jnp.dot(joined, out_buf[...], preferred_element_type=F32).astype(BF16)

    gathers = len(started)
    for turn in range(1, heads_dev):
        send(
            partials.at[my_head], partials.at[my_head], (me, head_peer(turn)), part_send.at[turn], part_recv.at[turn]
        )
    for copy in started[:gathers]:
        copy.wait_send()
    for hop in range(outer):
        for turn in range(1, heads_dev):
            group_copy(hop, turn).wait_send()
    for turn in range(1, heads_dev):
        source = lax.rem(my_head + heads_dev - turn, heads_dev)
        arrived(partials.at[source], part_recv.at[turn])
    total = partials[0].astype(F32)
    for index in range(1, heads_dev):
        total = total + partials[index].astype(F32)
    result[...] = total.astype(BF16)
    for copy in started[gathers:]:
        copy.wait_send()


def per_device(nodes, heads_dev, features, proj_weight, score_source, score_target, out_weight, presence, tile_masks):
    tile = features.shape[0]
    heads, width = score_source.shape
    slots = tile_masks.shape[1]
    outputs = out_weight.shape[1]
    inner = 1
    while inner * inner * 4 <= nodes:
        inner *= 2
    outer = nodes // inner
    assert outer & (outer - 1) == 0
    pad = -(-heads // 8) * 8
    sizes = (outer, inner, heads_dev, heads, width, tile, slots)
    dma = pltpu.SemaphoreType.DMA
    return pl.pallas_call(
        functools.partial(kernel, sizes),
        out_shape=jax.ShapeDtypeStruct((tile, outputs), BF16),
        in_specs=[pl.BlockSpec(memory_space=pltpu.HBM)] * 7,
        out_specs=pl.BlockSpec(memory_space=pltpu.VMEM),
        scratch_shapes=[
            pltpu.VMEM((nodes, tile // heads_dev, features.shape[1]), BF16),
            pltpu.VMEM((heads_dev - 1, nodes, tile // heads_dev, features.shape[1]), BF16),
            pltpu.VMEM(features.shape, BF16),
            pltpu.VMEM(proj_weight.shape, BF16),
            pltpu.VMEM((2, heads, width), F32),
            pltpu.VMEM(out_weight.shape, BF16),
            pltpu.SMEM(presence.shape, jnp.int32),
            pltpu.VMEM(tile_masks.shape[1:], jnp.int32),
            pltpu.VMEM((tile, slots * tile), F32),
            pltpu.VMEM((2, pad, heads * width), F32),
            pltpu.VMEM((tile, heads * width), BF16),
            pltpu.VMEM((slots * tile, heads * width), BF16),
            pltpu.VMEM((heads_dev, tile, outputs), BF16),
            dma((8,)),
            dma((outer,)),
            dma((outer,)),
            dma((outer, inner)),
            dma((outer, inner)),
            dma((outer, heads_dev)),
            dma((outer, heads_dev)),
            dma((heads_dev,)),
            dma((heads_dev,)),
        ],
        compiler_params=pltpu.CompilerParams(
            collective_id=0, has_side_effects=True, vmem_limit_bytes=48 * 1024 * 1024
        ),
        cost_estimate=pl.CostEstimate(
            flops=2 * tile * heads * width * (features.shape[1] + outputs)
            + 2 * slots * tile * heads * width * (features.shape[1] + tile),
            bytes_accessed=4 * slots * tile * tile + 2 * nodes * tile * features.shape[1],
            transcendentals=slots * tile * tile * heads,
        ),
    )(
        *(
            pltpu.with_memory_space_constraint(operand, pltpu.HBM)
            for operand in (features, proj_weight, score_source, score_target, out_weight, presence, tile_masks)
        )
    )


def solution(mesh):
    return jax.shard_map(
        functools.partial(per_device, mesh.shape["node"], mesh.shape["head"]),
        mesh=mesh,
        in_specs=(
            P("node", None),
            P(None, "head"),
            P("head", None),
            P("head", None),
            P("head", None),
            P("node", None),
            P("node", None, None, None),
        ),
        out_specs=P("node", None),
        check_vma=False,
    )
```
